512 devices in a mesh: section: 32 (over z_hi, x, core), dp: 16 (over z_lo, y).
Axes of the slice: x: 4, y: 8, z: 8 (z_hi: 4, z_lo: 2; z = z_hi * 2 + z_lo), core: 2. Of those that a mesh axis runs over, the one named last changes fastest.
Arguments:
- adapter_in: bfloat16 [32, 8192, 64], P('section', 'dp'), may hold values from -0.0625 to 0.0625
- adapter_out: bfloat16 [32, 64, 8192], P('section', None, 'dp'), may hold values from -0.375 to 0.375
- down_state: bfloat16 [32, 256, 8192], P('section', 'dp'), may hold values from -6 to 6
- up_state: bfloat16 [32, 256, 8192], P('section', 'dp'), may hold values from -6 to 6
- down_cot: bfloat16 [32, 256, 8192], P('section', 'dp'), may hold values from -6 to 6
- up_cot: bfloat16 [32, 256, 8192], P('section', 'dp'), may hold values from -6 to 6
- down_stash: bfloat16 [32, 3, 256, 8192], P('section', None, 'dp'), may hold values from -6 to 6
- up_stash: bfloat16 [32, 3, 256, 8192], P('section', None, 'dp'), may hold values from -6 to 6
- entering: bfloat16 [2, 2, 256, 8192], P(None, None, 'dp'), may hold values from -6 to 6
Outputs:
- down_out: bfloat16 [32, 256, 8192], P('section', 'dp')
- up_out: bfloat16 [32, 256, 8192], P('section', 'dp')
- down_back: bfloat16 [32, 256, 8192], P('section', 'dp')
- up_back: bfloat16 [32, 256, 8192], P('section', 'dp')
- grad_in: float32 [32, 8192, 64], P('section', 'dp')
- grad_out: float32 [32, 64, 8192], P('section', None, 'dp')
The draws below stay inside these ranges and needn't reach their ends.
All inputs are finite; a program needn't handle non-finite values.
Results may differ from the reference program's by a relative error of at most 0.019.
Values may be sent and summed in bfloat16 or wider, within the bound.
No kernel may reach another device: no remote copies, remote signals or barrier semaphores. Data moves between devices by JAX's collectives and lax.ppermute only.
A program may use at most 64 MiB of HBM per device.

```python
import jax
import jax.numpy as jnp
from jax import lax

D = 8192
RANK = 64
TICKS = 3
LAYERS = 32
ROWS = 256
N_DP = 16


def steps_of(rng, shape, cuts, least, largest):
    def one(dim, blocks):
        draws = jax.random.uniform(jax.random.fold_in(jax.random.fold_in(rng, 6), dim), (blocks,), jnp.float32, least / len(cuts), largest / len(cuts))
        return jnp.repeat(jnp.exp(draws), shape[dim] // blocks).reshape((-1,) + (1,) * (len(shape) - dim - 1))

    factor_of = one(*cuts[0])
    for cut in cuts[1:]:
        factor_of = factor_of * one(*cut)
    return factor_of


def normal_values(key, dims, scale, reach, cuts=(), dtype=jnp.bfloat16):
    entries = jax.random.normal(key, dims, jnp.float32) * scale
    if len(cuts) > 0:
        entries = steps_of(key, dims, cuts, -0.22, 0.18) * entries
    return jnp.clip(entries, min=-reach, max=reach).astype(dtype)


def setup_inputs(seed: int = 0) -> dict:
    keys = jax.random.split(jax.random.key(seed), 10)
    return {
        "adapter_in": normal_values(keys[0], (LAYERS, D, RANK), D ** -0.5, 0.0625, ((0, 32), (1, 16))),
        "adapter_out": normal_values(keys[1], (LAYERS, RANK, D), (4 * RANK) ** -0.5, 0.375, ((0, 32), (2, 16))),
        "down_state": normal_values(keys[2], (LAYERS, ROWS, D), 1.0, 6.0, ((0, 32), (1, 16))),
        "up_state": normal_values(keys[3], (LAYERS, ROWS, D), 1.0, 6.0, ((0, 32), (1, 16))),
        "down_cot": normal_values(keys[4], (LAYERS, ROWS, D), 1.0, 6.0, ((0, 32), (1, 16))),
        "up_cot": normal_values(keys[5], (LAYERS, ROWS, D), 1.0, 6.0, ((0, 32), (1, 16))),
        "down_stash": normal_values(keys[6], (LAYERS, TICKS, ROWS, D), 1.0, 6.0, ((0, 32), (2, 16))),
        "up_stash": normal_values(keys[7], (LAYERS, TICKS, ROWS, D), 1.0, 6.0, ((0, 32), (2, 16))),
        "entering": normal_values(keys[8], (2, TICKS - 1, ROWS, D), 1.0, 6.0, ((2, 16),)),
    }


epsilon = 1e-05

def pieces(rows, cot, w_in, w_out):
    x_wide = rows.astype(jnp.float32)
    inv_rms = lax.rsqrt(lax.optimization_barrier(jnp.mean(x_wide * x_wide, axis=-1, keepdims=True)) + epsilon)
    normed = x_wide * inv_rms
    normed_low = normed.astype(jnp.bfloat16)
    pre_act = jnp.dot(normed_low, w_in, preferred_element_type=jnp.float32)
    sigma = jax.nn.sigmoid(pre_act)
    hidden = (pre_act * sigma).astype(jnp.bfloat16)
    hidden_grad = lax.dot_general(cot, w_out, (((1,), (1,)), ((), ())), preferred_element_type=jnp.float32)
    pre_grad = (hidden_grad * sigma * (1.0 + pre_act * (1.0 - sigma))).astype(jnp.bfloat16)
    return (inv_rms, normed, normed_low, hidden, pre_grad)

def forward(rows, w_in, w_out):
    x_wide = rows.astype(jnp.float32)
    inv_rms = lax.rsqrt(lax.optimization_barrier(jnp.mean(x_wide * x_wide, axis=-1, keepdims=True)) + epsilon)
    normed_low = (x_wide * inv_rms).astype(jnp.bfloat16)
    pre_act = jnp.dot(normed_low, w_in, preferred_element_type=jnp.float32)
    hidden = (pre_act * jax.nn.sigmoid(pre_act)).astype(jnp.bfloat16)
    return (x_wide + jnp.dot(hidden, w_out, preferred_element_type=jnp.float32)).astype(jnp.bfloat16)

def input_grad(rows, cot, w_in, w_out):
    inv_rms, normed, normed_low, hidden, pre_grad = pieces(rows, cot, w_in, w_out)
    normed_grad = lax.dot_general(pre_grad, w_in, (((1,), (1,)), ((), ())), preferred_element_type=jnp.float32)
    inner = lax.optimization_barrier(jnp.mean(normed_grad * normed, axis=-1, keepdims=True))
    return (cot.astype(jnp.float32) + inv_rms * (normed_grad - normed * inner)).astype(jnp.bfloat16)

def replica_terms(rows, cots, w_in, w_out):
    ticks, total, width = rows.shape
    inv_rms, normed, normed_low, hidden, pre_grad = pieces(rows.reshape(ticks * total, width), cots.reshape(ticks * total, width), w_in, w_out)
    per_rep = total // N_DP
    normed_r = normed_low.astype(jnp.float32).reshape(ticks, N_DP, per_rep, width)
    pre_r = pre_grad.astype(jnp.float32).reshape(ticks, N_DP, per_rep, -1)
    hidden_r = hidden.astype(jnp.float32).reshape(ticks, N_DP, per_rep, -1)
    cot_r = cots.astype(jnp.float32).reshape(ticks, N_DP, per_rep, width)
    term_in = jnp.einsum('tkmd,tkmr->kdr', normed_r, pre_r, precision=lax.Precision.HIGHEST)
    term_out = jnp.einsum('tkmr,tkmd->krd', hidden_r, cot_r, precision=lax.Precision.HIGHEST)
    term_in = lax.optimization_barrier(term_in.astype(jnp.bfloat16)).astype(jnp.float32)
    term_out = lax.optimization_barrier(term_out.astype(jnp.bfloat16)).astype(jnp.float32)
    return (lax.optimization_barrier(jnp.sum(term_in, axis=0)), lax.optimization_barrier(jnp.sum(term_out, axis=0)))

def reference(adapter_in, adapter_out, down_state, up_state, down_cot, up_cot, down_stash, up_stash, entering):
    in_up = adapter_in[::-1]
    out_up = adapter_out[::-1]
    run_fwd = jax.vmap(forward)
    run_back = jax.vmap(input_grad)
    x_down, x_up, c_down, c_up = (down_state, up_state, down_cot, up_cot)
    keep_xd, keep_cd, keep_xu, keep_cu = ([], [], [], [])
    for moment in range(TICKS):
        y_down = run_fwd(x_down, adapter_in, adapter_out)
        y_up = run_fwd(x_up, in_up, out_up)
        xb_down = jnp.concatenate([down_stash[:-1, moment], x_down[-1:]], axis=0)
        cb_down = jnp.concatenate([c_down[:-1], y_down[-1:]], axis=0)
        xb_up = jnp.concatenate([x_up[:1], up_stash[1:, moment]], axis=0)
        cb_up = jnp.concatenate([y_up[:1], c_up[1:]], axis=0)
        g_down = run_back(xb_down, cb_down, adapter_in, adapter_out)
        g_up = run_back(xb_up, cb_up, in_up, out_up)
        keep_xd.append(xb_down)
        keep_cd.append(cb_down)
        keep_xu.append(xb_up)
        keep_cu.append(cb_up)
        if moment + 1 < TICKS:
            x_down = jnp.concatenate([entering[0, moment][None], y_down[:-1]], axis=0)
            x_up = jnp.concatenate([y_up[1:], entering[1, moment][None]], axis=0)
            c_down = jnp.concatenate([g_down[1:], jnp.zeros_like(g_down[:1])], axis=0)
            c_up = jnp.concatenate([jnp.zeros_like(g_up[:1]), g_up[:-1]], axis=0)
    stack_xd = jnp.stack(keep_xd, axis=1)
    stack_cd = jnp.stack(keep_cd, axis=1)
    stack_xu = jnp.stack(keep_xu, axis=1)[::-1]
    stack_cu = jnp.stack(keep_cu, axis=1)[::-1]

    def layer_grads(item):
        xd_rows, cd_rows, xu_rows, cu_rows, w_in, w_out = item
        in_down, out_down = replica_terms(xd_rows, cd_rows, w_in, w_out)
        in_upper, out_upper = replica_terms(xu_rows, cu_rows, w_in, w_out)
        return (in_down + in_upper, out_down + out_upper)
    grad_in, grad_out = lax.map(layer_grads, (stack_xd, stack_cd, stack_xu, stack_cu, adapter_in, adapter_out))
    return (y_down, y_up, g_down, g_up, grad_in, grad_out)
```

```python
import functools

import jax
import jax.numpy as jnp
from jax import lax
from jax.experimental import pallas as pl
from jax.experimental.pallas import tpu as pltpu
from jax.sharding import PartitionSpec as P

TICKS = 3
EPSILON = 1e-05
BF16 = jnp.bfloat16
F32 = jnp.float32

VMEM = pl.BlockSpec(memory_space=pltpu.VMEM)
SMEM = pl.BlockSpec(memory_space=pltpu.SMEM)
PARAMS = pltpu.CompilerParams(vmem_limit_bytes=40 * 2**20)


def nt(a, b):
    return lax.dot_general(a, b, (((1,), (1,)), ((), ())), preferred_element_type=F32)


def nn(a, b):
    return jnp.dot(a, b, preferred_element_type=F32)


def tn(a, b):
    return lax.dot_general(a, b, (((0,), (0,)), ((), ())), preferred_element_type=F32)


def both(parts, cols):
    if len(parts) == 1:
        return parts[0][:, cols]
    return jnp.concatenate([part[:, cols] for part in parts], axis=0)


def project(take, w_ref, half, square):
    blocks, _, wide = w_ref.shape
    rank = w_ref.shape[1] // 2
    total, squares = None, None
    for j in range(blocks):
        x = take(pl.ds(j * wide, wide))
        term = nt(x, w_ref[j, half * rank : (half + 1) * rank, :])
        total = term if total is None else total + term
        if square:
            x = x.astype(F32)
            squares = x * x if squares is None else squares + x * x
    if not square:
        return total
    return total, jnp.sum(squares, axis=-1, keepdims=True)


def forward_kernel(n_parts, flags, *refs):
    parts, rest = refs[:n_parts], refs[n_parts:]
    if n_parts == 1:
        enter_ref, w_ref, y_ref = rest
        first = flags[0] == 1

        def take(cols):
            entering = jnp.concatenate([enter_ref[0, :, cols], enter_ref[1, :, cols]], axis=0)
            return jnp.where(first, entering, parts[0][:, cols])
    else:
        w_ref, y_ref = rest

        def take(cols):
            return both(parts, cols)

    blocks, _, wide = w_ref.shape
    rank = w_ref.shape[1] // 2
    total, squares = project(take, w_ref, 0, True)
    inv_rms = lax.rsqrt(squares / (blocks * wide) + EPSILON)
    pre = total * inv_rms
    hidden = (pre * jax.nn.sigmoid(pre)).astype(BF16)
    for j in range(blocks):
        cols = pl.ds(j * wide, wide)
        y_ref[:, cols] = (take(cols).astype(F32) + nn(hidden, w_ref[j, rank:, :])).astype(BF16)


def backward_kernel(n_x, n_c, moment, flags, sd_ref, su_ref, *refs):
    xs, y_ref, refs = refs[:n_x], refs[n_x], refs[n_x + 1 :]
    cs, (w_ref, g_ref, pre_grad_ref, hidden_ref) = refs[:n_c], refs[n_c:]
    blocks, _, wide = w_ref.shape
    rank = w_ref.shape[1] // 2
    last = flags[1] == 1

    def rows(cols):
        stash = jnp.concatenate([sd_ref[moment, :, cols], su_ref[moment, :, cols]], axis=0)
        return jnp.where(last, both(xs, cols), stash)

    def cot(cols):
        return jnp.where(last, y_ref[:, cols], both(cs, cols))

    total, squares = project(rows, w_ref, 0, True)
    hidden_grad = project(cot, w_ref, 1, False)
    inv_rms = lax.rsqrt(squares / (blocks * wide) + EPSILON)
    pre = total * inv_rms
    sigma = jax.nn.sigmoid(pre)
    hidden_ref[...] = (pre * sigma).astype(BF16)
    pre_grad = (hidden_grad * sigma * (1.0 + pre * (1.0 - sigma))).astype(BF16)
    wide_grad = pre_grad.astype(F32)
    pre_grad_ref[...] = (wide_grad * inv_rms).astype(BF16)
    inner = jnp.sum(wide_grad * pre, axis=-1, keepdims=True) / (blocks * wide)
    back = inv_rms * inv_rms * inner
    for j in range(blocks):
        cols = pl.ds(j * wide, wide)
        normed_grad = nn(pre_grad, w_ref[j, :rank, :])
        g_ref[:, cols] = (
            cot(cols).astype(F32) + inv_rms * normed_grad - back * rows(cols).astype(F32)
        ).astype(BF16)


def terms_kernel(flags, sd_ref, su_ref, *refs):
    xd, xu, cd, cu, x1, x2, c1, c2, y0, y1, y2 = refs[:11]
    pre_grads, hiddens, out_ref = refs[11:14], refs[14:17], refs[17]
    blocks, _, wide = out_ref.shape
    rank = out_ref.shape[1] // 2
    last = flags[1] == 1
    pre_grad = jnp.concatenate([r[...] for r in pre_grads], axis=0)
    hidden = jnp.concatenate([r[...] for r in hiddens], axis=0)
    for j in range(blocks):
        cols = pl.ds(j * wide, wide)
        stash = jnp.concatenate([r[t, :, cols] for t in range(TICKS) for r in (sd_ref, su_ref)], axis=0)
        x = jnp.concatenate([r[:, cols] for r in (xd, xu, x1, x2)], axis=0)
        y = jnp.concatenate([r[:, cols] for r in (y0, y1, y2)], axis=0)
        c = jnp.concatenate([r[:, cols] for r in (cd, cu, c1, c2)], axis=0)
        out_ref[j, :rank, :] = tn(pre_grad, jnp.where(last, x, stash)).astype(BF16)
        out_ref[j, rank:, :] = tn(hidden, jnp.where(last, y, c)).astype(BF16)


def sum_kernel(rank, in_ref, a_ref, b_ref):
    total = in_ref[0].astype(F32)
    for j in range(1, in_ref.shape[0]):
        total = total + in_ref[j].astype(F32)
    a_ref[...] = total[:rank]
    b_ref[...] = total[rank:]


def call(kernel, out, *args, flops=0):
    specs = [SMEM if a.dtype == jnp.int32 else VMEM for a in args]
    outs = out if isinstance(out, (list, tuple)) else [out]
    size = sum(a.size * a.dtype.itemsize for a in list(args) + list(outs))
    return pl.pallas_call(
        kernel,
        out_shape=out,
        in_specs=specs,
        out_specs=jax.tree.map(lambda _: VMEM, out),
        compiler_params=PARAMS,
        cost_estimate=pl.CostEstimate(flops=flops, bytes_accessed=size, transcendentals=0),
    )(*args)


def body(
    adapter_in, adapter_out, down_state, up_state, down_cot, up_cot, down_stash, up_stash, entering
):
    sections = lax.axis_size("section")
    position = lax.axis_index("section")
    flags = jnp.stack([position == 0, position == sections - 1]).astype(jnp.int32)
    mirror = [(s, sections - 1 - s) for s in range(sections)]
    higher = [(s, s + 1) for s in range(sections - 1)]
    lower = [(s + 1, s) for s in range(sections - 1)]
    replicas = lax.axis_size("dp")
    share, rank = adapter_in.shape[1:]
    rows, width = down_state.shape[1:]
    shape = jax.ShapeDtypeStruct

    xd, cd, sd = down_state[0], down_cot[0], down_stash[0]
    xu = lax.ppermute(up_state[0], "section", mirror)
    cu = lax.ppermute(up_cot[0], "section", mirror)
    su = lax.ppermute(up_stash[0], "section", mirror)

    shard = jnp.concatenate([adapter_in[0].T, adapter_out[0]], axis=0)
    weights = lax.all_to_all(
        jnp.broadcast_to(shard[None], (replicas,) + shard.shape), "dp", 0, 0, tiled=True
    )

    one = 2 * 2 * rows * width * rank
    full = shape((2 * rows, width), BF16)
    low = shape((2 * rows, rank), BF16)
    x, c = (xd, xu), (cd, cu)
    xs, ys, cs, pre_grads, hiddens = [], [], [], [], []
    for moment in range(TICKS):
        enter = () if moment == 0 else (entering[:, moment - 1],)
        y = call(
            functools.partial(forward_kernel, len(x)), full, flags, *x, *enter, weights, flops=2 * one
        )
        g, pre_grad, hidden = call(
            functools.partial(backward_kernel, len(x), len(c), moment),
            [full, low, low],
            flags, sd, su, *x, y, *c, weights,
            flops=3 * one,
        )
        xs.append(x)
        ys.append(y)
        cs.append(c)
        pre_grads.append(pre_grad)
        hiddens.append(hidden)
        if moment + 1 < TICKS:
            x = (lax.ppermute(y, "section", higher),)
            c = (lax.ppermute(g, "section", lower),)
    partial = call(
        terms_kernel,
        shape((replicas, 2 * rank, share), BF16),
        flags, sd, su, *xs[0], *cs[0], *xs[1], *xs[2], *cs[1], *cs[2], *ys, *pre_grads, *hiddens,
        flops=6 * one,
    )
    up_out = lax.ppermute(y[rows:], "section", mirror)
    up_back = lax.ppermute(g[rows:], "section", mirror)
    pieces = lax.all_to_all(partial, "dp", 0, 0, tiled=True)
    grad_in, grad_out = call(
        functools.partial(sum_kernel, rank), [shape((rank, share), F32), shape((rank, share), F32)], pieces
    )
    return (y[None, :rows], up_out[None], g[None, :rows], up_back[None], grad_in.T[None], grad_out[None])


def solution(mesh):
    return jax.shard_map(
        body,
        mesh=mesh,
        in_specs=(
            P("section", "dp", None),
            P("section", None, "dp"),
            P("section", "dp", None),
            P("section", "dp", None),
            P("section", "dp", None),
            P("section", "dp", None),
            P("section", None, "dp", None),
            P("section", None, "dp", None),
            P(None, None, "dp", None),
        ),
        out_specs=(
            P("section", "dp", None),
            P("section", "dp", None),
            P("section", "dp", None),
            P("section", "dp", None),
            P("section", "dp", None),
            P("section", None, "dp"),
        ),
        check_vma=False,
    )
```

```python
import functools

import jax
import jax.numpy as jnp
from jax import lax
from jax.experimental import pallas as pl
from jax.experimental.pallas import tpu as pltpu
from jax.sharding import PartitionSpec as P

TICKS = 3
EPSILON = 1e-05
BF16 = jnp.bfloat16
F32 = jnp.float32

VMEM = pl.BlockSpec(memory_space=pltpu.VMEM)
SMEM = pl.BlockSpec(memory_space=pltpu.SMEM)
PLAIN = pl.BlockSpec()
PARAMS = pltpu.CompilerParams(vmem_limit_bytes=40 * 2**20)


def nt(a, b):
    return lax.dot_general(a, b, (((1,), (1,)), ((), ())), preferred_element_type=F32)


def nn(a, b):
    return jnp.dot(a, b, preferred_element_type=F32)


def tn(a, b):
    return lax.dot_general(a, b, (((0,), (0,)), ((), ())), preferred_element_type=F32)


def both(parts, spot, cols):
    if len(parts) == 1:
        return parts[0][:, cols]
    return jnp.concatenate([parts[0][:, cols], parts[1][spot, :, cols]], axis=0)


def stacked(refs, cols):
    return jnp.concatenate([ref[:, cols] for ref in refs], axis=0)


def put(refs, cols, value):
    count = value.shape[0] // len(refs)
    for i, ref in enumerate(refs):
        ref[:, cols] = value[i * count : (i + 1) * count]


def project(take, w_ref, half, square):
    blocks, _, wide = w_ref.shape
    rank = w_ref.shape[1] // 2
    total, squares = None, None
    for j in range(blocks):
        x = take(pl.ds(j * wide, wide))
        term = nt(x, w_ref[j, half * rank : (half + 1) * rank, :])
        total = term if total is None else total + term
        if square:
            x = x.astype(F32)
            squares = x * x if squares is None else squares + x * x
    if not square:
        return total
    return total, jnp.sum(squares, axis=-1, keepdims=True)


def forward_kernel(n_parts, flags, *refs):
    parts, rest = refs[:n_parts], refs[n_parts:]
    if n_parts == 1:
        enter_ref, w_ref, *y_refs = rest
        first = flags[0] == 1

        def take(cols):
            entering = jnp.concatenate([enter_ref[0, :, cols], enter_ref[1, :, cols]], axis=0)
            return jnp.where(first, entering, parts[0][:, cols])
    else:
        w_ref, *y_refs = rest

        def take(cols):
            return both(parts, 0, cols)

    blocks, _, wide = w_ref.shape
    rank = w_ref.shape[1] // 2
    total, squares = project(take, w_ref, 0, True)
    inv_rms = lax.rsqrt(squares / (blocks * wide) + EPSILON)
    pre = total * inv_rms
    hidden = (pre * jax.nn.sigmoid(pre)).astype(BF16)
    for j in range(blocks):
        cols = pl.ds(j * wide, wide)
        put(y_refs, cols, (take(cols).astype(F32) + nn(hidden, w_ref[j, rank:, :])).astype(BF16))


def backward_kernel(n_x, n_y, n_c, moment, spot, flags, sd_ref, su_ref, *refs):
    xs, ys, refs = refs[:n_x], refs[n_x : n_x + n_y], refs[n_x + n_y :]
    cs, (w_ref, pre_grad_ref, hidden_ref, *g_refs) = refs[:n_c], refs[n_c:]
    blocks, _, wide = w_ref.shape
    rank = w_ref.shape[1] // 2
    last = flags[1] == 1

    def rows(cols):
        stash = jnp.concatenate([sd_ref[moment, :, cols], su_ref[spot, :, cols]], axis=0)
        return jnp.where(last, both(xs, 0, cols), stash)

    def cot(cols):
        return jnp.where(last, stacked(ys, cols), both(cs, 0, cols))

    total, squares = project(rows, w_ref, 0, True)
    hidden_grad = project(cot, w_ref, 1, False)
    inv_rms = lax.rsqrt(squares / (blocks * wide) + EPSILON)
    pre = total * inv_rms
    sigma = jax.nn.sigmoid(pre)
    hidden_ref[...] = (pre * sigma).astype(BF16)
    pre_grad = (hidden_grad * sigma * (1.0 + pre * (1.0 - sigma))).astype(BF16)
    wide_grad = pre_grad.astype(F32)
    pre_grad_ref[...] = (wide_grad * inv_rms).astype(BF16)
    inner = jnp.sum(wide_grad * pre, axis=-1, keepdims=True) / (blocks * wide)
    back = inv_rms * inv_rms * inner
    for j in range(blocks):
        cols = pl.ds(j * wide, wide)
        normed_grad = nn(pre_grad, w_ref[j, :rank, :])
        g = cot(cols).astype(F32) + inv_rms * normed_grad - back * rows(cols).astype(F32)
        put(g_refs, cols, g.astype(BF16))


def terms_kernel(flags, sd_ref, first_ref, later_ref, *refs):
    xd, xu, cd, cu, x1, x2, c1, c2, y0, y1, y2_down, y2_up = refs[:12]
    pre_grads, hiddens, out_ref = refs[12:15], refs[15:18], refs[18]
    blocks, rank, wide = out_ref.shape
    rank = rank // 2
    last = flags[1] == 1
    pre_grad = jnp.concatenate([r[...] for r in pre_grads], axis=0)
    hidden = jnp.concatenate([r[...] for r in hiddens], axis=0)
    for j in range(blocks):
        cols = pl.ds(j * wide, wide)
        stash = jnp.concatenate(
            [sd_ref[0, :, cols], first_ref[0, :, cols], sd_ref[1, :, cols], later_ref[0, :, cols]]
            + [sd_ref[2, :, cols], later_ref[1, :, cols]],
            axis=0,
        )
        x = jnp.concatenate([xd[:, cols], xu[0, :, cols], x1[:, cols], x2[:, cols]], axis=0)
        y = stacked((y0, y1, y2_down, y2_up), cols)
        c = jnp.concatenate([cd[:, cols], cu[0, :, cols], c1[:, cols], c2[:, cols]], axis=0)
        out_ref[j, :rank, :] = tn(pre_grad, jnp.where(last, x, stash)).astype(BF16)
        out_ref[j, rank:, :] = tn(hidden, jnp.where(last, y, c)).astype(BF16)


def sum_kernel(rank, in_ref, y_ref, g_ref, a_ref, b_ref, y_out, g_out):
    total = in_ref[0].astype(F32)
    for j in range(1, in_ref.shape[0]):
        total = total + in_ref[j].astype(F32)
    a_ref[...] = total[:rank]
    b_ref[...] = total[rank:]
    y_out[...] = y_ref[...]
    g_out[...] = g_ref[...]


def call(kernel, out, *args, flops=0, out_specs=None):
    specs = [SMEM if a.dtype == jnp.int32 else VMEM for a in args]
    outs = out if isinstance(out, (list, tuple)) else [out]
    size = sum(a.size * a.dtype.itemsize for a in list(args) + list(outs))
    return pl.pallas_call(
        kernel,
        out_shape=out,
        in_specs=specs,
        out_specs=jax.tree.map(lambda _: VMEM, out) if out_specs is None else out_specs,
        compiler_params=PARAMS,
        cost_estimate=pl.CostEstimate(flops=flops, bytes_accessed=size, transcendentals=0),
    )(*args)


def body(
    adapter_in, adapter_out, down_state, up_state, down_cot, up_cot, down_stash, up_stash, entering
):
    sections = lax.axis_size("section")
    position = lax.axis_index("section")
    flags = jnp.stack([position == 0, position == sections - 1]).astype(jnp.int32)
    mirror = [(s, sections - 1 - s) for s in range(sections)]
    higher = [(s, s + 1) for s in range(sections - 1)]
    lower = [(s + 1, s) for s in range(sections - 1)]
    replicas = lax.axis_size("dp")
    share, rank = adapter_in.shape[1:]
    rows, width = down_state.shape[1:]
    shape = jax.ShapeDtypeStruct

    xd, cd, sd = down_state[0], down_cot[0], down_stash[0]
    first = lax.ppermute(up_stash[0, 0], "section", mirror)
    xu = lax.ppermute(up_state[0], "section", mirror)
    cu = lax.ppermute(up_cot[0], "section", mirror)
    later = lax.ppermute(up_stash[0, 1:], "section", mirror)
    su = [first[None], later, later]
    spots = [0, 0, 1]

    shard = jnp.concatenate([adapter_in[0].T, adapter_out[0]], axis=0)
    weights = lax.all_to_all(
        jnp.broadcast_to(shard[None], (replicas,) + shard.shape), "dp", 0, 0, tiled=True
    )

    x0, c0 = xu[None], cu[None]
    one = 2 * 2 * rows * width * rank
    full = shape((2 * rows, width), BF16)
    half = shape((rows, width), BF16)
    low = shape((2 * rows, rank), BF16)
    x, c = (xd, xu[None]), (cd, cu[None])
    xs, ys, cs, pre_grads, hiddens = [], [], [], [], []
    for moment in range(TICKS):
        enter = () if moment == 0 else (entering[:, moment - 1],)
        ends = moment + 1 == TICKS
        outs, plain = ([half, half], [PLAIN, PLAIN]) if ends else ([full], [VMEM])
        y = call(
            functools.partial(forward_kernel, len(x)),
            outs, flags, *x, *enter, weights,
            flops=2 * one, out_specs=plain,
        )
        pre_grad, hidden, *g = call(
            functools.partial(backward_kernel, len(x), len(y), len(c), moment, spots[moment]),
            [low, low] + outs,
            flags, sd, su[moment], *x, *y, *c, weights,
            flops=3 * one, out_specs=[VMEM, VMEM] + plain,
        )
        xs.append(x)
        ys.append(y)
        cs.append(c)
        pre_grads.append(pre_grad)
        hiddens.append(hidden)
        if moment + 1 < TICKS:
            x = (lax.ppermute(y[0], "section", higher),)
            c = (lax.ppermute(g[0], "section", lower),)
    partial = call(
        terms_kernel,
        shape((replicas, 2 * rank, share), BF16),
        flags, sd, su[0], later, xd, x0, cd, c0, *xs[1], *xs[2], *cs[1], *cs[2], *ys[0], *ys[1], *ys[2], *pre_grads, *hiddens,
        flops=6 * one,
    )
    up_out = lax.ppermute(y[1], "section", mirror)
    up_back = lax.ppermute(g[1], "section", mirror)
    pieces = lax.all_to_all(partial, "dp", 0, 0, tiled=True)
    piece = shape((rank, share), F32)
    grad_in, grad_out, up_out, up_back = call(
        functools.partial(sum_kernel, rank), [piece, piece, half, half], pieces, up_out, up_back, out_specs=[PLAIN] * 4
    )
    return (y[0][None], up_out[None], g[0][None], up_back[None], grad_in.T[None], grad_out[None])


def solution(mesh):
    return jax.shard_map(
        body,
        mesh=mesh,
        in_specs=(
            P("section", "dp", None),
            P("section", None, "dp"),
            P("section", "dp", None),
            P("section", "dp", None),
            P("section", "dp", None),
            P("section", "dp", None),
            P("section", None, "dp", None),
            P("section", None, "dp", None),
            P(None, None, "dp", None),
        ),
        out_specs=(
            P("section", "dp", None),
            P("section", "dp", None),
            P("section", "dp", None),
            P("section", "dp", None),
            P("section", "dp", None),
            P("section", None, "dp"),
        ),
        check_vma=False,
    )
```

```python
import functools

import jax
import jax.numpy as jnp
from jax import lax
from jax.experimental import pallas as pl
from jax.experimental.pallas import tpu as pltpu
from jax.sharding import PartitionSpec as P

TICKS = 3
EPSILON = 1e-05
BF16 = jnp.bfloat16
F32 = jnp.float32

VMEM = pl.BlockSpec(memory_space=pltpu.VMEM)
SMEM = pl.BlockSpec(memory_space=pltpu.SMEM)
PARAMS = pltpu.CompilerParams(vmem_limit_bytes=40 * 2**20)


def nt(a, b):
    return lax.dot_general(a, b, (((1,), (1,)), ((), ())), preferred_element_type=F32)


def nn(a, b):
    return jnp.dot(a, b, preferred_element_type=F32)


def tn(a, b):
    return lax.dot_general(a, b, (((0,), (0,)), ((), ())), preferred_element_type=F32)


def join_kernel(a_ref, b_ref, c_ref, out_ref, kept_ref):
    n = a_ref.shape[0]
    out_ref[:n] = a_ref[...]
    out_ref[n:] = b_ref[...]
    kept_ref[...] = c_ref[...]


def both(parts, spot, cols):
    if len(parts) == 1:
        return parts[0][:, cols]
    return jnp.concatenate([parts[0][:, cols], parts[1][spot, :, cols]], axis=0)


def project(take, w_ref, half, square):
    blocks, _, wide = w_ref.shape
    rank = w_ref.shape[1] // 2
    total, squares = None, None
    for j in range(blocks):
        x = take(pl.ds(j * wide, wide))
        term = nt(x, w_ref[j, half * rank : (half + 1) * rank, :])
        total = term if total is None else total + term
        if square:
            x = x.astype(F32)
            squares = x * x if squares is None else squares + x * x
    if not square:
        return total
    return total, jnp.sum(squares, axis=-1, keepdims=True)


def forward_kernel(n_parts, flags, *refs):
    parts, rest = refs[:n_parts], refs[n_parts:]
    if len(rest) == 3:
        enter_ref, w_ref, y_ref = rest
        first = flags[0] == 1

        def take(cols):
            entering = jnp.concatenate([enter_ref[0, :, cols], enter_ref[1, :, cols]], axis=0)
            return jnp.where(first, entering, parts[0][:, cols])
    else:
        w_ref, y_ref = rest

        def take(cols):
            return both(parts, 0, cols)

    blocks, _, wide = w_ref.shape
    rank = w_ref.shape[1] // 2
    total, squares = project(take, w_ref, 0, True)
    inv_rms = lax.rsqrt(squares / (blocks * wide) + EPSILON)
    pre = total * inv_rms
    hidden = (pre * jax.nn.sigmoid(pre)).astype(BF16)
    for j in range(blocks):
        cols = pl.ds(j * wide, wide)
        y_ref[:, cols] = (take(cols).astype(F32) + nn(hidden, w_ref[j, rank:, :])).astype(BF16)


def backward_kernel(n_x, n_c, moment, spot, flags, sd_ref, su_ref, *refs):
    xs, y_ref, refs = refs[:n_x], refs[n_x], refs[n_x + 1 :]
    cs, (w_ref, g_ref, pre_grad_ref, hidden_ref) = refs[:n_c], refs[n_c:]
    blocks, _, wide = w_ref.shape
    rank = w_ref.shape[1] // 2
    last = flags[1] == 1

    def rows(cols):
        stash = jnp.concatenate([sd_ref[moment, :, cols], su_ref[spot, :, cols]], axis=0)
        return jnp.where(last, both(xs, 0, cols), stash)

    def cot(cols):
        return jnp.where(last, y_ref[:, cols], both(cs, 0, cols))

    total, squares = project(rows, w_ref, 0, True)
    hidden_grad = project(cot, w_ref, 1, False)
    inv_rms = lax.rsqrt(squares / (blocks * wide) + EPSILON)
    pre = total * inv_rms
    sigma = jax.nn.sigmoid(pre)
    hidden_ref[...] = (pre * sigma).astype(BF16)
    pre_grad = (hidden_grad * sigma * (1.0 + pre * (1.0 - sigma))).astype(BF16)
    wide_grad = pre_grad.astype(F32)
    pre_grad_ref[...] = (wide_grad * inv_rms).astype(BF16)
    inner = jnp.sum(wide_grad * pre, axis=-1, keepdims=True) / (blocks * wide)
    back = inv_rms * inv_rms * inner
    for j in range(blocks):
        cols = pl.ds(j * wide, wide)
        normed_grad = nn(pre_grad, w_ref[j, :rank, :])
        g_ref[:, cols] = (
            cot(cols).astype(F32) + inv_rms * normed_grad - back * rows(cols).astype(F32)
        ).astype(BF16)


def terms_kernel(flags, sd_ref, first_ref, later_ref, *refs):
    x0, cd, cu, x1, x2, c1, c2, y0, y1, y2 = refs[:10]
    pre_grads, hiddens, out_ref = refs[10:13], refs[13:16], refs[16]
    blocks, _, wide = out_ref.shape
    rank = out_ref.shape[1] // 2
    last = flags[1] == 1
    pre_grad = jnp.concatenate([r[...] for r in pre_grads], axis=0)
    hidden = jnp.concatenate([r[...] for r in hiddens], axis=0)
    for j in range(blocks):
        cols = pl.ds(j * wide, wide)
        stash = jnp.concatenate(
            [sd_ref[0, :, cols], first_ref[0, :, cols], sd_ref[1, :, cols], later_ref[0, :, cols]]
            + [sd_ref[2, :, cols], later_ref[1, :, cols]],
            axis=0,
        )
        x = jnp.concatenate([x0[:, cols], x1[:, cols], x2[:, cols]], axis=0)
        y = jnp.concatenate([r[:, cols] for r in (y0, y1, y2)], axis=0)
        c = jnp.concatenate([cd[:, cols], cu[0, :, cols], c1[:, cols], c2[:, cols]], axis=0)
        out_ref[j, :rank, :] = tn(pre_grad, jnp.where(last, x, stash)).astype(BF16)
        out_ref[j, rank:, :] = tn(hidden, jnp.where(last, y, c)).astype(BF16)


def sum_kernel(rank, in_ref, a_ref, b_ref):
    total = in_ref[0].astype(F32)
    for j in range(1, in_ref.shape[0]):
        total = total + in_ref[j].astype(F32)
    a_ref[...] = total[:rank]
    b_ref[...] = total[rank:]


def call(kernel, out, *args, flops=0):
    specs = [SMEM if a.dtype == jnp.int32 else VMEM for a in args]
    outs = out if isinstance(out, (list, tuple)) else [out]
    size = sum(a.size * a.dtype.itemsize for a in list(args) + list(outs))
    return pl.pallas_call(
        kernel,
        out_shape=out,
        in_specs=specs,
        out_specs=jax.tree.map(lambda _: VMEM, out),
        compiler_params=PARAMS,
        cost_estimate=pl.CostEstimate(flops=flops, bytes_accessed=size, transcendentals=0),
    )(*args)


def body(
    adapter_in, adapter_out, down_state, up_state, down_cot, up_cot, down_stash, up_stash, entering
):
    sections = lax.axis_size("section")
    position = lax.axis_index("section")
    flags = jnp.stack([position == 0, position == sections - 1]).astype(jnp.int32)
    mirror = [(s, sections - 1 - s) for s in range(sections)]
    higher = [(s, s + 1) for s in range(sections - 1)]
    lower = [(s + 1, s) for s in range(sections - 1)]
    replicas = lax.axis_size("dp")
    share, rank = adapter_in.shape[1:]
    rows, width = down_state.shape[1:]
    shape = jax.ShapeDtypeStruct

    xd, cd, sd = down_state[0], down_cot[0], down_stash[0]
    first = lax.ppermute(up_stash[0, 0], "section", mirror)
    xu = lax.ppermute(up_state[0], "section", mirror)
    cu = lax.ppermute(up_cot[0], "section", mirror)
    later = lax.ppermute(up_stash[0, 1:], "section", mirror)
    su = [first[None], later, later]
    spots = [0, 0, 1]

    shard = jnp.concatenate([adapter_in[0].T, adapter_out[0]], axis=0)
    weights = lax.all_to_all(
        jnp.broadcast_to(shard[None], (replicas,) + shard.shape), "dp", 0, 0, tiled=True
    )

    one = 2 * 2 * rows * width * rank
    full = shape((2 * rows, width), BF16)
    low = shape((2 * rows, rank), BF16)
    x0, cu = call(join_kernel, [full, shape(cu.shape, BF16)], xd, xu, cu)
    c0 = cu[None]
    x, c = (x0,), (cd, c0)
    xs, ys, cs, pre_grads, hiddens = [], [], [], [], []
    for moment in range(TICKS):
        enter = () if moment == 0 else (entering[:, moment - 1],)
        y = call(
            functools.partial(forward_kernel, len(x)), full, flags, *x, *enter, weights, flops=2 * one
        )
        g, pre_grad, hidden = call(
            functools.partial(backward_kernel, len(x), len(c), moment, spots[moment]),
            [full, low, low],
            flags, sd, su[moment], *x, y, *c, weights,
            flops=3 * one,
        )
        xs.append(x)
        ys.append(y)
        cs.append(c)
        pre_grads.append(pre_grad)
        hiddens.append(hidden)
        if moment + 1 < TICKS:
            x = (lax.ppermute(y, "section", higher),)
            c = (lax.ppermute(g, "section", lower),)
    partial = call(
        terms_kernel,
        shape((replicas, 2 * rank, share), BF16),
        flags, sd, su[0], later, x0, cd, c0, *xs[1], *xs[2], *cs[1], *cs[2], *ys, *pre_grads, *hiddens,
        flops=6 * one,
    )
    up_out = lax.ppermute(y[rows:], "section", mirror)
    up_back = lax.ppermute(g[rows:], "section", mirror)
    pieces = lax.all_to_all(partial, "dp", 0, 0, tiled=True)
    grad_in, grad_out = call(
        functools.partial(sum_kernel, rank), [shape((rank, share), F32), shape((rank, share), F32)], pieces
    )
    return (y[None, :rows], up_out[None], g[None, :rows], up_back[None], grad_in.T[None], grad_out[None])


def solution(mesh):
    return jax.shard_map(
        body,
        mesh=mesh,
        in_specs=(
            P("section", "dp", None),
            P("section", None, "dp"),
            P("section", "dp", None),
            P("section", "dp", None),
            P("section", "dp", None),
            P("section", "dp", None),
            P("section", None, "dp", None),
            P("section", None, "dp", None),
            P(None, None, "dp", None),
        ),
        out_specs=(
            P("section", "dp", None),
            P("section", "dp", None),
            P("section", "dp", None),
            P("section", "dp", None),
            P("section", "dp", None),
            P("section", None, "dp"),
        ),
        check_vma=False,
    )
```

```python
import functools

import jax
import jax.numpy as jnp
from jax import lax
from jax.experimental import pallas as pl
from jax.experimental.pallas import tpu as pltpu
from jax.sharding import PartitionSpec as P

TICKS = 3
EPSILON = 1e-05
BF16 = jnp.bfloat16
F32 = jnp.float32

VMEM = pl.BlockSpec(memory_space=pltpu.VMEM)
SMEM = pl.BlockSpec(memory_space=pltpu.SMEM)
PLAIN = pl.BlockSpec()
PARAMS = pltpu.CompilerParams(vmem_limit_bytes=40 * 2**20)


def nt(a, b):
    return lax.dot_general(a, b, (((1,), (1,)), ((), ())), preferred_element_type=F32)


def nn(a, b):
    return jnp.dot(a, b, preferred_element_type=F32)


def tn(a, b):
    return lax.dot_general(a, b, (((0,), (0,)), ((), ())), preferred_element_type=F32)


def both(parts, spot, cols):
    if len(parts) == 1:
        return parts[0][:, cols]
    return jnp.concatenate([parts[0][:, cols], parts[1][spot, :, cols]], axis=0)


def stacked(refs, cols):
    return jnp.concatenate([ref[:, cols] for ref in refs], axis=0)


def put(refs, cols, value):
    count = value.shape[0] // len(refs)
    for i, ref in enumerate(refs):
        ref[:, cols] = value[i * count : (i + 1) * count]


def project(take, w_ref, half, square):
    blocks, _, wide = w_ref.shape
    rank = w_ref.shape[1] // 2
    total, squares = None, None
    for j in range(blocks):
        x = take(pl.ds(j * wide, wide))
        term = nt(x, w_ref[j, half * rank : (half + 1) * rank, :])
        total = term if total is None else total + term
        if square:
            x = x.astype(F32)
            squares = x * x if squares is None else squares + x * x
    if not square:
        return total
    return total, jnp.sum(squares, axis=-1, keepdims=True)


def forward_kernel(n_parts, flags, *refs):
    parts, rest = refs[:n_parts], refs[n_parts:]
    if n_parts == 1:
        enter_ref, w_ref, *y_refs = rest
        first = flags[0] == 1

        def take(cols):
            entering = jnp.concatenate([enter_ref[0, :, cols], enter_ref[1, :, cols]], axis=0)
            return jnp.where(first, entering, parts[0][:, cols])
    else:
        w_ref, *y_refs = rest

        def take(cols):
            return both(parts, 0, cols)

    blocks, _, wide = w_ref.shape
    rank = w_ref.shape[1] // 2
    total, squares = project(take, w_ref, 0, True)
    inv_rms = lax.rsqrt(squares / (blocks * wide) + EPSILON)
    pre = total * inv_rms
    hidden = (pre * jax.nn.sigmoid(pre)).astype(BF16)
    for j in range(blocks):
        cols = pl.ds(j * wide, wide)
        put(y_refs, cols, (take(cols).astype(F32) + nn(hidden, w_ref[j, rank:, :])).astype(BF16))


def backward_kernel(n_x, n_y, n_c, moment, spot, flags, sd_ref, su_ref, *refs):
    xs, ys, refs = refs[:n_x], refs[n_x : n_x + n_y], refs[n_x + n_y :]
    cs, (w_ref, pre_grad_ref, hidden_ref, *g_refs) = refs[:n_c], refs[n_c:]
    blocks, _, wide = w_ref.shape
    rank = w_ref.shape[1] // 2
    last = flags[1] == 1

    def rows(cols):
        stash = jnp.concatenate([sd_ref[moment, :, cols], su_ref[spot, :, cols]], axis=0)
        return jnp.where(last, both(xs, 0, cols), stash)

    def cot(cols):
        return jnp.where(last, stacked(ys, cols), both(cs, 0, cols))

    total, squares = project(rows, w_ref, 0, True)
    hidden_grad = project(cot, w_ref, 1, False)
    inv_rms = lax.rsqrt(squares / (blocks * wide) + EPSILON)
    pre = total * inv_rms
    sigma = jax.nn.sigmoid(pre)
    hidden_ref[...] = (pre * sigma).astype(BF16)
    pre_grad = (hidden_grad * sigma * (1.0 + pre * (1.0 - sigma))).astype(BF16)
    wide_grad = pre_grad.astype(F32)
    pre_grad_ref[...] = (wide_grad * inv_rms).astype(BF16)
    inner = jnp.sum(wide_grad * pre, axis=-1, keepdims=True) / (blocks * wide)
    back = inv_rms * inv_rms * inner
    for j in range(blocks):
        cols = pl.ds(j * wide, wide)
        normed_grad = nn(pre_grad, w_ref[j, :rank, :])
        g = cot(cols).astype(F32) + inv_rms * normed_grad - back * rows(cols).astype(F32)
        put(g_refs, cols, g.astype(BF16))


def terms_kernel(flags, sd_ref, later_ref, *refs):
    xd, xu, cd, cu, x1, x2, c1, c2, y0, y1, y2_down, y2_up = refs[:12]
    pre_grads, hiddens, out_ref = refs[12:15], refs[15:18], refs[18]
    blocks, rank, wide = out_ref.shape
    rank = rank // 2
    last = flags[1] == 1
    pre_grad = jnp.concatenate([r[...] for r in pre_grads], axis=0)
    hidden = jnp.concatenate([r[...] for r in hiddens], axis=0)
    for j in range(blocks):
        cols = pl.ds(j * wide, wide)
        stash = jnp.concatenate(
            [sd_ref[0, :, cols], cu[1, :, cols], sd_ref[1, :, cols], later_ref[0, :, cols]]
            + [sd_ref[2, :, cols], later_ref[1, :, cols]],
            axis=0,
        )
        x = jnp.concatenate([xd[:, cols], xu[0, :, cols], x1[:, cols], x2[:, cols]], axis=0)
        y = stacked((y0, y1, y2_down, y2_up), cols)
        c = jnp.concatenate([cd[:, cols], cu[0, :, cols], c1[:, cols], c2[:, cols]], axis=0)
        out_ref[j, :rank, :] = tn(pre_grad, jnp.where(last, x, stash)).astype(BF16)
        out_ref[j, rank:, :] = tn(hidden, jnp.where(last, y, c)).astype(BF16)


def sum_kernel(rank, in_ref, y_ref, g_ref, a_ref, b_ref, y_out, g_out):
    total = in_ref[0].astype(F32)
    for j in range(1, in_ref.shape[0]):
        total = total + in_ref[j].astype(F32)
    a_ref[...] = total[:rank]
    b_ref[...] = total[rank:]
    y_out[...] = y_ref[...]
    g_out[...] = g_ref[...]


def call(kernel, out, *args, flops=0, out_specs=None):
    specs = [SMEM if a.dtype == jnp.int32 else VMEM for a in args]
    outs = out if isinstance(out, (list, tuple)) else [out]
    size = sum(a.size * a.dtype.itemsize for a in list(args) + list(outs))
    return pl.pallas_call(
        kernel,
        out_shape=out,
        in_specs=specs,
        out_specs=jax.tree.map(lambda _: VMEM, out) if out_specs is None else out_specs,
        compiler_params=PARAMS,
        cost_estimate=pl.CostEstimate(flops=flops, bytes_accessed=size, transcendentals=0),
    )(*args)


def body(
    adapter_in, adapter_out, down_state, up_state, down_cot, up_cot, down_stash, up_stash, entering
):
    sections = lax.axis_size("section")
    position = lax.axis_index("section")
    flags = jnp.stack([position == 0, position == sections - 1]).astype(jnp.int32)
    mirror = [(s, sections - 1 - s) for s in range(sections)]
    higher = [(s, s + 1) for s in range(sections - 1)]
    lower = [(s + 1, s) for s in range(sections - 1)]
    replicas = lax.axis_size("dp")
    share, rank = adapter_in.shape[1:]
    rows, width = down_state.shape[1:]
    shape = jax.ShapeDtypeStruct

    xd, cd, sd = down_state[0], down_cot[0], down_stash[0]
    xu = lax.ppermute(up_state[0], "section", mirror)
    cu = lax.ppermute(jnp.stack([up_cot[0], up_stash[0, 0]]), "section", mirror)
    later = lax.ppermute(up_stash[0, 1:], "section", mirror)
    su = [cu, later, later]
    spots = [1, 0, 1]

    shard = jnp.concatenate([adapter_in[0].T, adapter_out[0]], axis=0)
    weights = lax.all_to_all(
        jnp.broadcast_to(shard[None], (replicas,) + shard.shape), "dp", 0, 0, tiled=True
    )

    x0 = xu[None]
    one = 2 * 2 * rows * width * rank
    full = shape((2 * rows, width), BF16)
    half = shape((rows, width), BF16)
    low = shape((2 * rows, rank), BF16)
    x, c = (xd, xu[None]), (cd, cu)
    xs, ys, cs, pre_grads, hiddens = [], [], [], [], []
    for moment in range(TICKS):
        enter = () if moment == 0 else (entering[:, moment - 1],)
        ends = moment + 1 == TICKS
        outs, plain = ([half, half], [PLAIN, PLAIN]) if ends else ([full], [VMEM])
        y = call(
            functools.partial(forward_kernel, len(x)),
            outs, flags, *x, *enter, weights,
            flops=2 * one, out_specs=plain,
        )
        pre_grad, hidden, *g = call(
            functools.partial(backward_kernel, len(x), len(y), len(c), moment, spots[moment]),
            [low, low] + outs,
            flags, sd, su[moment], *x, *y, *c, weights,
            flops=3 * one, out_specs=[VMEM, VMEM] + plain,
        )
        xs.append(x)
        ys.append(y)
        cs.append(c)
        pre_grads.append(pre_grad)
        hiddens.append(hidden)
        if moment + 1 < TICKS:
            x = (lax.ppermute(y[0], "section", higher),)
            c = (lax.ppermute(g[0], "section", lower),)
    partial = call(
        terms_kernel,
        shape((replicas, 2 * rank, share), BF16),
        flags, sd, later, xd, x0, cd, cu, *xs[1], *xs[2], *cs[1], *cs[2], *ys[0], *ys[1], *ys[2], *pre_grads, *hiddens,
        flops=6 * one,
    )
    up_out = lax.ppermute(y[1], "section", mirror)
    up_back = lax.ppermute(g[1], "section", mirror)
    pieces = lax.all_to_all(partial, "dp", 0, 0, tiled=True)
    piece = shape((rank, share), F32)
    grad_in, grad_out, up_out, up_back = call(
        functools.partial(sum_kernel, rank), [piece, piece, half, half], pieces, up_out, up_back, out_specs=[PLAIN] * 4
    )
    return (y[0][None], up_out[None], g[0][None], up_back[None], grad_in.T[None], grad_out[None])


def solution(mesh):
    return jax.shard_map(
        body,
        mesh=mesh,
        in_specs=(
            P("section", "dp", None),
            P("section", None, "dp"),
            P("section", "dp", None),
            P("section", "dp", None),
            P("section", "dp", None),
            P("section", "dp", None),
            P("section", None, "dp", None),
            P("section", None, "dp", None),
            P(None, None, "dp", None),
        ),
        out_specs=(
            P("section", "dp", None),
            P("section", "dp", None),
            P("section", "dp", None),
            P("section", "dp", None),
            P("section", "dp", None),
            P("section", None, "dp"),
        ),
        check_vma=False,
    )
```
